32 devices in a mesh: dp: 8 (over z, x), ctx: 4 (over y, core).
Axes of the slice: x: 2, y: 2, z: 4, core: 2. Of those that a mesh axis runs over, the one named last changes fastest.
Arguments:
- tokens: bfloat16 [16, 1024, 1024], P('dp', 'ctx'), may hold values from -6 to 6
- doc_lengths: int32 [16, 3], P('dp'), may hold values from 1 to 1022, as said below
- in_gain: bfloat16 [1024], P(('dp', 'ctx')), may hold values from 0.25 to 1.75
- w_query: bfloat16 [1024, 2048], P(('dp', 'ctx')), may hold values from -0.1875 to 0.1875
- w_key: bfloat16 [1024, 1024], P(('dp', 'ctx')), may hold values from -0.1875 to 0.1875
- w_value: bfloat16 [1024, 1024], P(('dp', 'ctx')), may hold values from -0.1875 to 0.1875
- q_gain: bfloat16 [128], P(('dp', 'ctx')), may hold values from 0.25 to 1.75
- k_gain: bfloat16 [128], P(('dp', 'ctx')), may hold values from 0.25 to 1.75
- w_out: bfloat16 [2048, 1024], P(('dp', 'ctx')), may hold values from -1 to 1
- post_gain: bfloat16 [1024], P(('dp', 'ctx')), may hold values from 0.25 to 1.75
- w_gate: bfloat16 [1024, 3072], P(('dp', 'ctx')), may hold values from -0.1875 to 0.1875
- w_up: bfloat16 [1024, 3072], P(('dp', 'ctx')), may hold values from -0.1875 to 0.1875
- w_down: bfloat16 [3072, 1024], P(('dp', 'ctx')), may hold values from -0.109375 to 0.109375
- cotangent: bfloat16 [16, 1024, 1024], P('dp', 'ctx'), may hold values from -6 to 6
Outputs:
- mixed: bfloat16 [16, 1024, 1024], P('dp', 'ctx')
- tokens_grad: float32 [16, 1024, 1024], P('dp', 'ctx')
- in_gain_grad: float32 [1024], P(('dp', 'ctx'))
- w_query_grad: float32 [1024, 2048], P(('dp', 'ctx'))
- w_key_grad: float32 [1024, 1024], P(('dp', 'ctx'))
- w_value_grad: float32 [1024, 1024], P(('dp', 'ctx'))
- q_gain_grad: float32 [128], P(('dp', 'ctx'))
- k_gain_grad: float32 [128], P(('dp', 'ctx'))
- w_out_grad: float32 [2048, 1024], P(('dp', 'ctx'))
- post_gain_grad: float32 [1024], P(('dp', 'ctx'))
- w_gate_grad: float32 [1024, 3072], P(('dp', 'ctx'))
- w_up_grad: float32 [1024, 3072], P(('dp', 'ctx'))
- w_down_grad: float32 [3072, 1024], P(('dp', 'ctx'))
The draws below stay inside these ranges and needn't reach their ends.
Inputs may be any that keep to these rules, and one draw needn't show every extreme that they name: `doc_lengths`: each row holds three document lengths that sum to 1024; the first and the last are each under 256, so the middle document holds tokens of every device along ctx.
All inputs are finite; a program needn't handle non-finite values.
Results may differ from the reference program's by a relative error of at most 0.02.
Values may be sent and summed in bfloat16 or wider, within the bound.
A program may use at most 256 MiB of HBM per device.

```python
import math
import jax
import jax.numpy as jnp
from jax import lax

D = 1024
HEADS = 16
KV_HEADS = 8
HD = 128
FF = 3072
SEQ_LEN = 1024
SEQ_DEV = 256
SEQUENCES = 16


def draw_doc_lengths(key, part):
    key = jax.random.fold_in(key, 7)
    first_key, last_key, row_key = jax.random.split(key, 3)
    first_len = jax.random.randint(first_key, (SEQUENCES,), 1, SEQ_DEV)
    last_len = jax.random.randint(last_key, (SEQUENCES,), 1, SEQ_DEV)
    chosen = jax.random.randint(row_key, (), 0, SEQUENCES)
    row_ids = jnp.arange(SEQUENCES)
    first_len = jnp.where(row_ids == chosen, 1, first_len)
    last_len = jnp.where(row_ids == chosen, 1, last_len)
    middle = SEQ_LEN - first_len - last_len
    return jnp.stack([first_len, middle, last_len], axis=1).astype(jnp.int32)


def level_of(own_key, dims, cuts, smallest, high):
    loudness = 1.0
    for position, blocks in cuts:
        steps = jax.random.uniform(jax.random.fold_in(jax.random.fold_in(own_key, 6), position), (blocks,), jnp.float32, smallest / len(cuts), high / len(cuts))
        loudness = loudness * jnp.repeat(jnp.exp(steps), dims[position] // blocks).reshape((-1,) + (1,) * (len(dims) - 1 - position))
    return loudness


def bell_draw(stream_key, extent, deviation, bound, cuts=(), held_as=jnp.bfloat16):
    level = level_of(stream_key, extent, cuts, -0.22, 0.18) if cuts else 1.0
    values = jax.random.normal(stream_key, extent, jnp.float32) * deviation * level
    return jnp.minimum(jnp.maximum(values, -bound), bound).astype(held_as)


def setup_inputs(seed: int = 0) -> dict:
    arg_keys = jax.random.split(jax.random.key(seed), 15)
    return {
        "tokens": bell_draw(arg_keys[0], (SEQUENCES, SEQ_LEN, D), 1.0, 6.0, ((0, 8), (1, 4))),
        "doc_lengths": draw_doc_lengths(jax.random.fold_in(arg_keys[14], 71), 0),
        "in_gain": jnp.clip(1.0 + 0.15 * jax.random.normal(arg_keys[2], (D,), jnp.float32), 0.25, 1.75).astype(jnp.bfloat16),
        "w_query": bell_draw(arg_keys[3], (D, HEADS * HD), D ** -0.5, 0.1875, ((0, 32),)),
        "w_key": bell_draw(arg_keys[4], (D, KV_HEADS * HD), D ** -0.5, 0.1875, ((0, 32),)),
        "w_value": bell_draw(arg_keys[5], (D, KV_HEADS * HD), D ** -0.5, 0.1875, ((0, 32),)),
        "q_gain": jnp.clip(1.0 + 0.15 * jax.random.normal(arg_keys[6], (HD,), jnp.float32), 0.25, 1.75).astype(jnp.bfloat16),
        "k_gain": jnp.clip(1.0 + 0.15 * jax.random.normal(arg_keys[7], (HD,), jnp.float32), 0.25, 1.75).astype(jnp.bfloat16),
        "w_out": bell_draw(arg_keys[8], (HEADS * HD, D), (HEADS * HD // 64) ** -0.5, 1.0, ((0, 32),)),
        "post_gain": jnp.clip(1.0 + 0.15 * jax.random.normal(arg_keys[9], (D,), jnp.float32), 0.25, 1.75).astype(jnp.bfloat16),
        "w_gate": bell_draw(arg_keys[10], (D, FF), D ** -0.5, 0.1875, ((0, 32),)),
        "w_up": bell_draw(arg_keys[11], (D, FF), D ** -0.5, 0.1875, ((0, 32),)),
        "w_down": bell_draw(arg_keys[12], (FF, D), FF ** -0.5, 0.109375, ((0, 32),)),
        "cotangent": bell_draw(arg_keys[13], (SEQUENCES, SEQ_LEN, D), 1.0, 6.0, ((0, 8), (1, 4))),
    }


@jax.custom_vjp
def low(v):
    return lax.optimization_barrier(v.astype(jnp.bfloat16)).astype(jnp.float32)

@jax.custom_vjp
def low_back(v):
    return v

def low_keep(v):
    return (low(v), None)

def low_pass(kept, grad):
    return (grad,)

def back_keep(v):
    return (v, None)

def back_low(kept, grad):
    return (low(grad),)
low.defvjp(low_keep, low_pass)
low_back.defvjp(back_keep, back_low)
EPSILON = 1e-06
THETA = 1000000.0
NEGATIVE = -1e+30
PRECISE = lax.Precision.HIGHEST

def rms_scale(values, gain):
    inverse = lax.rsqrt(lax.optimization_barrier(jnp.mean(values * values, axis=-1, keepdims=True)) + EPSILON)
    return values * inverse * gain

def doc_layout(row_lengths, positions):
    doc_ends = jnp.cumsum(row_lengths).astype(jnp.int32)
    passed = positions[:, None] >= doc_ends[None, :]
    segment = lax.optimization_barrier(jnp.sum(passed.astype(jnp.int32), axis=1)).astype(jnp.int32)
    doc_start = lax.optimization_barrier(jnp.sum(jnp.where(passed, row_lengths[None, :], 0), axis=1)).astype(jnp.int32)
    return (segment, (positions - doc_start).astype(jnp.int32))

def rope_tables(relative, head_dim):
    half_dim = head_dim // 2
    exponent = jnp.arange(half_dim, dtype=jnp.float32) * (2.0 / head_dim)
    inverse = jnp.exp(-math.log(THETA) * exponent)
    angles = relative.astype(jnp.float32)[..., None] * inverse
    return (jnp.cos(angles), jnp.sin(angles))

def rotate(values, cosine_table, sine_table):
    half_dim = values.shape[-1] // 2
    front_part = values[..., :half_dim]
    back_part = values[..., half_dim:]
    return jnp.concatenate([front_part * cosine_table - back_part * sine_table, back_part * cosine_table + front_part * sine_table], axis=-1)

def layer_one(inputs, segment, relative, weights):
    in_gain, w_query, w_key, w_value, q_gain, k_gain, w_out, post_gain, w_gate, w_up, w_down = weights
    seq_len = inputs.shape[0]
    head_dim = q_gain.shape[0]
    normed = low(rms_scale(inputs, in_gain))
    queries = low_back(jnp.dot(normed, w_query, precision=PRECISE))
    key_pre = low_back(jnp.dot(normed, w_key, precision=PRECISE))
    values = low(low_back(jnp.dot(normed, w_value, precision=PRECISE)))
    queries = queries.reshape(seq_len, -1, head_dim)
    key_pre = key_pre.reshape(seq_len, -1, head_dim)
    kv_heads = key_pre.shape[1]
    group_size = queries.shape[1] // kv_heads
    cosine_table, sine_table = rope_tables(relative, head_dim)
    cosine_table = cosine_table[:, None, :]
    sine_table = sine_table[:, None, :]
    q_rot = low(rotate(rms_scale(queries, q_gain), cosine_table, sine_table))
    k_rot = low(rotate(rms_scale(key_pre, k_gain), cosine_table, sine_table))
    grouped = q_rot.reshape(seq_len, kv_heads, group_size, head_dim)
    value_heads = values.reshape(seq_len, kv_heads, head_dim)
    scores = jnp.einsum('qkgd,skd->kgqs', grouped, k_rot, precision=PRECISE) * head_dim ** (-0.5)
    scores = low_back(scores)
    positions = jnp.arange(seq_len, dtype=jnp.int32)
    allowed = (segment[:, None] == segment[None, :]) & (positions[None, :] <= positions[:, None])
    scores = jnp.where(allowed, scores, NEGATIVE)
    attn_probs = low(jax.nn.softmax(scores, axis=-1))
    attended = jnp.einsum('kgqs,skd->qkgd', attn_probs, value_heads, precision=PRECISE).reshape(seq_len, -1)
    attended = low(low_back(attended))
    branch = low_back(jnp.dot(attended, w_out, precision=PRECISE))
    resid = inputs + branch
    normed_two = low(rms_scale(resid, post_gain))
    gate_pre = low_back(jnp.dot(normed_two, w_gate, precision=PRECISE))
    up_pre = low_back(jnp.dot(normed_two, w_up, precision=PRECISE))
    hidden = low(jax.nn.silu(gate_pre) * up_pre)
    mixed_part = low_back(jnp.dot(hidden, w_down, precision=PRECISE))
    return resid + mixed_part

def reference(tokens, doc_lengths, in_gain, w_query, w_key, w_value, q_gain, k_gain, w_out, post_gain, w_gate, w_up, w_down, cotangent):
    weights = tuple((item.astype(jnp.float32) for item in (in_gain, w_query, w_key, w_value, q_gain, k_gain, w_out, post_gain, w_gate, w_up, w_down)))
    inputs = tokens.astype(jnp.float32)
    positions = jnp.arange(tokens.shape[1], dtype=jnp.int32)
    segment, relative = jax.vmap(lambda row_lengths: doc_layout(row_lengths, positions))(doc_lengths)

    def forward(inputs, weights):
        step = jax.checkpoint(lambda seq_item: layer_one(seq_item[0], seq_item[1], seq_item[2], weights))
        return lax.map(step, (inputs, segment, relative))
    outputs, pullback = jax.vjp(forward, inputs, weights)
    input_grad, grads = pullback(cotangent.astype(jnp.float32))
    return (outputs.astype(jnp.bfloat16), input_grad, grads[0], grads[1], grads[2], grads[3], grads[4], grads[5], grads[6], grads[7], grads[8], grads[9], grads[10])
```

```python
import math

import jax
import jax.numpy as jnp
from jax import lax
from jax.sharding import PartitionSpec as P

EPSILON = 1e-06
THETA = 1000000.0
NEGATIVE = -1e30


def doc_layout(doc_lengths, positions):
    doc_ends = jnp.cumsum(doc_lengths, axis=1)
    passed = positions[None, :, None] >= doc_ends[:, None, :]
    segment = jnp.sum(passed.astype(jnp.int32), axis=2)
    doc_start = jnp.sum(jnp.where(passed, doc_lengths[:, None, :], 0), axis=2)
    return (segment, positions[None, :] - doc_start)


def rope_tables(relative, head_dim):
    half_dim = head_dim // 2
    exponent = jnp.arange(half_dim, dtype=jnp.float32) * (2.0 / head_dim)
    inverse = jnp.exp(-math.log(THETA) * exponent)
    angles = relative.astype(jnp.float32)[..., None] * inverse
    return (jnp.cos(angles), jnp.sin(angles))


def rotate(values, cosine_table, sine_table):
    half_dim = values.shape[-1] // 2
    front_part = values[..., :half_dim]
    back_part = values[..., half_dim:]
    return jnp.concatenate(
        [
            front_part * cosine_table - back_part * sine_table,
            back_part * cosine_table + front_part * sine_table,
        ],
        axis=-1,
    )


def unrotate(grads, cosine_table, sine_table):
    half_dim = grads.shape[-1] // 2
    front_part = grads[..., :half_dim]
    back_part = grads[..., half_dim:]
    return jnp.concatenate(
        [
            front_part * cosine_table + back_part * sine_table,
            back_part * cosine_table - front_part * sine_table,
        ],
        axis=-1,
    )


def norm_forward(values, gain):
    inverse = lax.rsqrt(jnp.mean(values * values, axis=-1, keepdims=True) + EPSILON)
    return (values * inverse * gain, inverse)


def norm_backward(values, inverse, gain, grad_out):
    scaled = grad_out * gain
    cubed = inverse * inverse * inverse
    value_grad = inverse * scaled - values * cubed * jnp.mean(
        scaled * values, axis=-1, keepdims=True
    )
    gain_grad = jnp.sum((grad_out * values * inverse).reshape(-1, values.shape[-1]), axis=0)
    return (value_grad, gain_grad)


def lead_product(left, right):
    return lax.dot_general(
        left, right, (((0,), (0,)), ((), ())), preferred_element_type=jnp.float32
    )


def tail_product(left, right):
    return lax.dot_general(
        left, right, (((1,), (1,)), ((), ())), preferred_element_type=jnp.float32
    )


AXES = ("dp", "ctx")


def bit_orders(count):
    bits = count.bit_length() - 1
    rest = list(range(1, bits))
    shift = max(1, (bits - 1) // 3)
    return [[0] + rest[shift * turn :] + rest[: shift * turn] for turn in range(3)]


def swap(block, axes, count, bit):
    pairs = [(device, device ^ (1 << bit)) for device in range(count)]
    return lax.ppermute(block, axes, pairs)


def scatter_sum(terms, axes, order, lead=1, out_type=jnp.float32):
    count = lax.axis_size(axes)
    me = lax.axis_index(axes)
    tail = (terms.shape[0] // (lead * count),) + terms.shape[1:]
    left = sorted(order, reverse=True)
    for step, bit in enumerate(order):
        place = left.index(bit)
        above = lead << place
        below = 1 << (len(left) - place - 1)
        left.remove(bit)
        split = terms.reshape((above, 2, below * tail[0]) + tail[1:])
        mine = (me >> bit) & 1
        away = lax.dynamic_index_in_dim(split, 1 - mine, 1, keepdims=False)
        keep = lax.dynamic_index_in_dim(split, mine, 1, keepdims=False)
        got = swap(away, axes, count, bit)
        total = keep.astype(jnp.float32) + got.astype(jnp.float32)
        terms = total.astype(out_type if step == len(order) - 1 else terms.dtype)
    return terms.reshape((lead * tail[0],) + tail[1:])


def gather_all(shard, axes, order, lead=1):
    count = lax.axis_size(axes)
    me = lax.axis_index(axes)
    tail = (shard.shape[0] // lead,) + shard.shape[1:]
    held = []
    block = shard
    for bit in reversed(order):
        got = swap(block, axes, count, bit)
        mine = (me >> bit) & 1
        held = sorted(held + [bit], reverse=True)
        place = held.index(bit)
        above = lead << place
        below = 1 << (len(held) - place - 1)
        shape = (above, 1, below * tail[0]) + tail[1:]
        own = block.reshape(shape)
        other = got.reshape(shape)
        first = jnp.where(mine == 0, own, other)
        second = jnp.where(mine == 0, other, own)
        block = jnp.concatenate([first, second], axis=1)
        block = block.reshape((lead * tail[0] << len(held),) + tail[1:])
    return block


def local(
    tokens,
    doc_lengths,
    in_gain,
    w_query,
    w_key,
    w_value,
    q_gain,
    k_gain,
    w_out,
    post_gain,
    w_gate,
    w_up,
    w_down,
    cotangent,
):
    count = lax.axis_size(AXES)
    orders = bit_orders(count)
    ctx_order = list(range(lax.axis_size("ctx").bit_length() - 1))
    gains = jnp.concatenate([in_gain, q_gain, k_gain, post_gain])
    gain_width = -(-gains.shape[0] // 128) * 128
    gains = jnp.pad(gains, (0, gain_width - gains.shape[0]))
    gains = gather_all(gains[None, :], AXES, orders[0])
    cuts = [in_gain.shape[0], q_gain.shape[0], k_gain.shape[0], post_gain.shape[0]]
    ends = [sum(cuts[: i + 1]) for i in range(4)]
    gain_one, qgain_full, kgain_full, gain_two = [
        gains[:, end - cut : end].reshape(-1) for cut, end in zip(cuts, ends)
    ]
    query_mat = gather_all(w_query, AXES, orders[1])
    key_mat = gather_all(w_key, AXES, orders[2])
    value_mat = gather_all(w_value, AXES, orders[0])
    out_mat = gather_all(w_out, AXES, orders[0])
    gate_mat = gather_all(w_gate, AXES, orders[1])
    up_mat = gather_all(w_up, AXES, orders[2])
    down_mat = gather_all(w_down, AXES, orders[0])
    seq_count, local_len, model_width = tokens.shape
    seq_len = local_len * lax.axis_size("ctx")
    head_dim = qgain_full.shape[0]
    kv_heads = key_mat.shape[1] // head_dim
    q_heads = query_mat.shape[1] // head_dim
    group_size = q_heads // kv_heads
    kv_width = kv_heads * head_dim
    row_count = seq_count * local_len
    score_scale = head_dim ** (-0.5)
    local_pos = lax.axis_index("ctx") * local_len + jnp.arange(local_len, dtype=jnp.int32)
    key_pos = jnp.arange(seq_len, dtype=jnp.int32)
    q_segment, q_relative = doc_layout(doc_lengths, local_pos)
    k_segment = doc_layout(doc_lengths, key_pos)[0]
    gain_in = gain_one.astype(jnp.float32)
    gain_query = qgain_full.astype(jnp.float32)
    gain_key = kgain_full.astype(jnp.float32)
    gain_post = gain_two.astype(jnp.float32)
    inputs = tokens.reshape(row_count, model_width).astype(jnp.float32)
    normed, inverse_one = norm_forward(inputs, gain_in)
    normed_low = normed.astype(jnp.bfloat16)
    queries = jnp.dot(normed_low, query_mat, preferred_element_type=jnp.float32).reshape(
        seq_count, local_len, q_heads, head_dim
    )
    key_pre = jnp.dot(normed_low, key_mat, preferred_element_type=jnp.float32).reshape(
        seq_count, local_len, kv_heads, head_dim
    )
    values_low = (
        jnp.dot(normed_low, value_mat, preferred_element_type=jnp.float32)
        .astype(jnp.bfloat16)
        .reshape(seq_count, local_len, kv_width)
    )
    cosine_table, sine_table = rope_tables(q_relative, head_dim)
    cosine_table = cosine_table[:, :, None, :]
    sine_table = sine_table[:, :, None, :]
    q_normed, q_inverse = norm_forward(queries, gain_query)
    q_low = rotate(q_normed, cosine_table, sine_table).astype(jnp.bfloat16)
    k_normed, k_inverse = norm_forward(key_pre, gain_key)
    k_low = (
        rotate(k_normed, cosine_table, sine_table)
        .astype(jnp.bfloat16)
        .reshape(seq_count, local_len, kv_width)
    )
    key_all = [gather_all(k_low[i], "ctx", ctx_order) for i in range(seq_count)]
    value_all = [gather_all(values_low[i], "ctx", ctx_order) for i in range(seq_count)]

    def block_scores(q_seq, k_seq, q_seg, k_seg, k_positions):
        grouped = q_seq.reshape(local_len, kv_heads, group_size, head_dim)
        key_heads = k_seq.reshape(k_seq.shape[0], kv_heads, head_dim)
        scores = score_scale * jnp.einsum(
            "qkgd,skd->kgqs", grouped, key_heads, preferred_element_type=jnp.float32
        )
        allowed = (q_seg[:, None] == k_seg[None, :]) & (k_positions[None, :] <= local_pos[:, None])
        return (jnp.where(allowed, scores, NEGATIVE), grouped, key_heads)

    def attend(seq_item):
        q_seq, k_seq, v_seq, q_seg, k_seg = seq_item
        scores, grouped, key_heads = block_scores(q_seq, k_seq, q_seg, k_seg, key_pos)
        value_heads = v_seq.reshape(seq_len, kv_heads, head_dim)
        row_peak = jnp.max(scores, axis=-1, keepdims=True)
        exp_scores = jnp.exp(scores - row_peak)
        row_total = jnp.sum(exp_scores, axis=-1, keepdims=True)
        probs_low = (exp_scores / row_total).astype(jnp.bfloat16)
        attended = jnp.einsum(
            "kgqs,skd->qkgd", probs_low, value_heads, preferred_element_type=jnp.float32
        )
        return (
            attended.reshape(local_len, q_heads * head_dim).astype(jnp.bfloat16),
            row_peak + jnp.log(row_total),
        )

    forward = [
        attend((q_low[i], key_all[i], value_all[i], q_segment[i], k_segment[i]))
        for i in range(seq_count)
    ]
    log_totals = [item[1] for item in forward]
    attended_flat = jnp.concatenate([item[0] for item in forward], axis=0)
    resid = inputs + jnp.dot(attended_flat, out_mat, preferred_element_type=jnp.float32)
    normed_two, inverse_two = norm_forward(resid, gain_post)
    normed_two_low = normed_two.astype(jnp.bfloat16)
    gate_pre = jnp.dot(normed_two_low, gate_mat, preferred_element_type=jnp.float32)
    up_pre = jnp.dot(normed_two_low, up_mat, preferred_element_type=jnp.float32)
    gate_sigmoid = jax.nn.sigmoid(gate_pre)
    gate_silu = gate_pre * gate_sigmoid
    hidden_low = (gate_silu * up_pre).astype(jnp.bfloat16)
    mixed = (resid + jnp.dot(hidden_low, down_mat, preferred_element_type=jnp.float32)).astype(
        jnp.bfloat16
    )
    grad_low = cotangent.reshape(row_count, model_width)
    w_down_grad = lead_product(hidden_low, grad_low)
    hidden_grad = tail_product(grad_low, down_mat)
    gate_grad = (
        hidden_grad * up_pre * gate_sigmoid * (1.0 + gate_pre * (1.0 - gate_sigmoid))
    ).astype(jnp.bfloat16)
    up_grad = (hidden_grad * gate_silu).astype(jnp.bfloat16)
    w_gate_grad = lead_product(normed_two_low, gate_grad)
    w_up_grad = lead_product(normed_two_low, up_grad)
    normed_two_grad = tail_product(gate_grad, gate_mat) + tail_product(up_grad, up_mat)
    resid_norm_grad, post_gain_grad = norm_backward(
        resid, inverse_two, gain_two.astype(jnp.float32), normed_two_grad
    )
    resid_grad = grad_low.astype(jnp.float32) + resid_norm_grad
    resid_low = resid_grad.astype(jnp.bfloat16)
    w_out_grad = lead_product(attended_flat, resid_low)
    attended_grad = (
        tail_product(resid_low, out_mat)
        .astype(jnp.bfloat16)
        .reshape(seq_count, local_len, q_heads * head_dim)
    )

    def score_terms(q_seq, k_seq, v_seq, q_seg, k_seg, k_positions, log_total, grad_seq):
        scores, grouped, key_heads = block_scores(q_seq, k_seq, q_seg, k_seg, k_positions)
        value_heads = v_seq.reshape(k_seq.shape[0], kv_heads, head_dim)
        attn_probs = jnp.exp(scores - log_total)
        grad_heads = grad_seq.reshape(local_len, kv_heads, group_size, head_dim)
        prob_grad = jnp.einsum(
            "qkgd,skd->kgqs", grad_heads, value_heads, preferred_element_type=jnp.float32
        )
        return (attn_probs, prob_grad, grouped, key_heads, grad_heads)

    def attend_back(seq_item):
        q_seq, k_seq, v_seq, q_seg, k_seg, log_total, grad_seq = seq_item
        attn_probs, prob_grad, grouped, key_heads, grad_heads = score_terms(
            q_seq, k_seq, v_seq, q_seg, k_seg, key_pos, log_total, grad_seq
        )
        probs_low = attn_probs.astype(jnp.bfloat16)
        row_dot = jnp.sum(attn_probs * prob_grad, axis=-1, keepdims=True)
        score_grad = (attn_probs * (prob_grad - row_dot)).astype(jnp.bfloat16)
        query_grad = score_scale * jnp.einsum(
            "kgqs,skd->qkgd", score_grad, key_heads, preferred_element_type=jnp.float32
        )
        key_grad = score_scale * jnp.einsum(
            "kgqs,qkgd->skd", score_grad, grouped, preferred_element_type=jnp.float32
        )
        value_grad = jnp.einsum(
            "kgqs,qkgd->skd", probs_low, grad_heads, preferred_element_type=jnp.float32
        )
        return (
            query_grad.reshape(local_len, q_heads, head_dim),
            key_grad.reshape(seq_len, kv_width),
            value_grad.reshape(seq_len, kv_width),
        )

    backward = [
        attend_back(
            (
                q_low[i],
                key_all[i],
                value_all[i],
                q_segment[i],
                k_segment[i],
                log_totals[i],
                attended_grad[i],
            )
        )
        for i in range(seq_count)
    ]
    q_rot_grad = jnp.stack([item[0] for item in backward])
    key_part, value_part = [
        jnp.stack(
            [scatter_sum(item[j].astype(jnp.bfloat16), "ctx", ctx_order) for item in backward]
        )
        for j in (1, 2)
    ]
    q_pre_grad, q_gain_grad = norm_backward(
        queries,
        q_inverse,
        qgain_full.astype(jnp.float32),
        unrotate(q_rot_grad, cosine_table, sine_table),
    )
    k_rot_grad = key_part.reshape(seq_count, local_len, kv_heads, head_dim)
    k_pre_grad, k_gain_grad = norm_backward(
        key_pre,
        k_inverse,
        kgain_full.astype(jnp.float32),
        unrotate(k_rot_grad, cosine_table, sine_table),
    )
    queries_grad = q_pre_grad.astype(jnp.bfloat16).reshape(row_count, q_heads * head_dim)
    keys_grad = k_pre_grad.astype(jnp.bfloat16).reshape(row_count, kv_width)
    values_low_grad = value_part.astype(jnp.bfloat16).reshape(row_count, kv_width)
    w_query_grad = lead_product(normed_low, queries_grad)
    w_key_grad = lead_product(normed_low, keys_grad)
    w_value_grad = lead_product(normed_low, values_low_grad)
    normed_grad = (
        tail_product(queries_grad, query_mat)
        + tail_product(keys_grad, key_mat)
        + tail_product(values_low_grad, value_mat)
    )
    input_norm_grad, in_gain_grad = norm_backward(
        inputs, inverse_one, gain_one.astype(jnp.float32), normed_grad
    )
    tokens_grad = (resid_grad + input_norm_grad).reshape(seq_count, local_len, model_width)
    gain_terms = jnp.concatenate(
        [
            part.reshape(count, -1)
            for part in (in_gain_grad, q_gain_grad, k_gain_grad, post_gain_grad)
        ],
        axis=1,
    )
    gain_terms = jnp.pad(gain_terms, ((0, 0), (0, gain_width - gain_terms.shape[1])))
    gain_sums = scatter_sum(gain_terms, AXES, orders[0])[0]
    in_gain_sum, q_gain_sum, k_gain_sum, post_gain_sum = [
        gain_sums[end - cut : end] for cut, end in zip(cuts, ends)
    ]
    return (
        mixed.reshape(seq_count, local_len, model_width),
        tokens_grad,
        in_gain_sum,
        scatter_sum(w_query_grad.astype(jnp.bfloat16), AXES, orders[1]),
        scatter_sum(w_key_grad.astype(jnp.bfloat16), AXES, orders[2]),
        scatter_sum(w_value_grad.astype(jnp.bfloat16), AXES, orders[0]),
        q_gain_sum,
        k_gain_sum,
        scatter_sum(w_out_grad.astype(jnp.bfloat16), AXES, orders[0]),
        post_gain_sum,
        scatter_sum(w_gate_grad.astype(jnp.bfloat16), AXES, orders[1]),
        scatter_sum(w_up_grad.astype(jnp.bfloat16), AXES, orders[2]),
        scatter_sum(w_down_grad.astype(jnp.bfloat16), AXES, orders[0]),
    )


def solution(mesh):
    placed = (
        P("dp", "ctx", None),
        P("dp", None),
        P(("dp", "ctx")),
        P(("dp", "ctx"), None),
        P(("dp", "ctx"), None),
        P(("dp", "ctx"), None),
        P(("dp", "ctx")),
        P(("dp", "ctx")),
        P(("dp", "ctx"), None),
        P(("dp", "ctx")),
        P(("dp", "ctx"), None),
        P(("dp", "ctx"), None),
        P(("dp", "ctx"), None),
        P("dp", "ctx", None),
    )
    return jax.shard_map(
        local,
        mesh=mesh,
        in_specs=placed,
        out_specs=(
            P("dp", "ctx", None),
            P("dp", "ctx", None),
            P(("dp", "ctx")),
            P(("dp", "ctx"), None),
            P(("dp", "ctx"), None),
            P(("dp", "ctx"), None),
            P(("dp", "ctx")),
            P(("dp", "ctx")),
            P(("dp", "ctx"), None),
            P(("dp", "ctx")),
            P(("dp", "ctx"), None),
            P(("dp", "ctx"), None),
            P(("dp", "ctx"), None),
        ),
        check_vma=False,
    )
```

```python
import math

import jax
import jax.numpy as jnp
from jax import lax
from jax.sharding import PartitionSpec as P

EPSILON = 1e-06
THETA = 1000000.0
NEGATIVE = -1e30


def doc_layout(doc_lengths, positions):
    doc_ends = jnp.cumsum(doc_lengths, axis=1)
    passed = positions[None, :, None] >= doc_ends[:, None, :]
    segment = jnp.sum(passed.astype(jnp.int32), axis=2)
    doc_start = jnp.sum(jnp.where(passed, doc_lengths[:, None, :], 0), axis=2)
    return (segment, positions[None, :] - doc_start)


def rope_tables(relative, head_dim):
    half_dim = head_dim // 2
    exponent = jnp.arange(half_dim, dtype=jnp.float32) * (2.0 / head_dim)
    inverse = jnp.exp(-math.log(THETA) * exponent)
    angles = relative.astype(jnp.float32)[..., None] * inverse
    return (jnp.cos(angles), jnp.sin(angles))


def rotate(values, cosine_table, sine_table):
    half_dim = values.shape[-1] // 2
    front_part = values[..., :half_dim]
    back_part = values[..., half_dim:]
    return jnp.concatenate(
        [
            front_part * cosine_table - back_part * sine_table,
            back_part * cosine_table + front_part * sine_table,
        ],
        axis=-1,
    )


def unrotate(grads, cosine_table, sine_table):
    half_dim = grads.shape[-1] // 2
    front_part = grads[..., :half_dim]
    back_part = grads[..., half_dim:]
    return jnp.concatenate(
        [
            front_part * cosine_table + back_part * sine_table,
            back_part * cosine_table - front_part * sine_table,
        ],
        axis=-1,
    )


def norm_forward(values, gain):
    inverse = lax.rsqrt(jnp.mean(values * values, axis=-1, keepdims=True) + EPSILON)
    return (values * inverse * gain, inverse)


def norm_backward(values, inverse, gain, grad_out):
    scaled = grad_out * gain
    cubed = inverse * inverse * inverse
    value_grad = inverse * scaled - values * cubed * jnp.mean(
        scaled * values, axis=-1, keepdims=True
    )
    gain_grad = jnp.sum((grad_out * values * inverse).reshape(-1, values.shape[-1]), axis=0)
    return (value_grad, gain_grad)


def lead_product(left, right):
    return lax.dot_general(
        left, right, (((0,), (0,)), ((), ())), preferred_element_type=jnp.float32
    )


def tail_product(left, right):
    return lax.dot_general(
        left, right, (((1,), (1,)), ((), ())), preferred_element_type=jnp.float32
    )


AXES = ("dp", "ctx")


def bit_orders(count):
    bits = count.bit_length() - 1
    rest = list(range(1, bits))
    shift = max(1, (bits - 1) // 3)
    return [[0] + rest[shift * turn :] + rest[: shift * turn] for turn in range(3)]


def swap(block, axes, count, bit):
    pairs = [(device, device ^ (1 << bit)) for device in range(count)]
    return lax.ppermute(block, axes, pairs)


def scatter_step(terms, axes, order, step, out_type):
    count = lax.axis_size(axes)
    mine = (lax.axis_index(axes) >> order[step]) & 1
    above = 1 << sorted(order[step:], reverse=True).index(order[step])
    split = terms.reshape((above, 2, terms.shape[0] // (2 * above)) + terms.shape[1:])
    away = lax.dynamic_index_in_dim(split, 1 - mine, 1, keepdims=False)
    keep = lax.dynamic_index_in_dim(split, mine, 1, keepdims=False)
    got = swap(away, axes, count, order[step])
    total = (keep.astype(jnp.float32) + got.astype(jnp.float32)).astype(out_type)
    return total.reshape((terms.shape[0] // 2,) + terms.shape[1:])


def scatter_sum(terms, axes, order, start=0):
    for step in range(start, len(order)):
        last = step == len(order) - 1
        terms = scatter_step(terms, axes, order, step, jnp.float32 if last else terms.dtype)
    return terms


def step_all(terms, orders, step):
    return [
        scatter_step(term, AXES, order, step, term.dtype) for term, order in zip(terms, orders)
    ]


def gather_all(shard, axes, order, lead=1):
    count = lax.axis_size(axes)
    me = lax.axis_index(axes)
    tail = (shard.shape[0] // lead,) + shard.shape[1:]
    held = []
    block = shard
    for bit in reversed(order):
        got = swap(block, axes, count, bit)
        mine = (me >> bit) & 1
        held = sorted(held + [bit], reverse=True)
        place = held.index(bit)
        above = lead << place
        below = 1 << (len(held) - place - 1)
        shape = (above, 1, below * tail[0]) + tail[1:]
        own = block.reshape(shape)
        other = got.reshape(shape)
        first = jnp.where(mine == 0, own, other)
        second = jnp.where(mine == 0, other, own)
        block = jnp.concatenate([first, second], axis=1)
        block = block.reshape((lead * tail[0] << len(held),) + tail[1:])
    return block


def local(
    tokens,
    doc_lengths,
    in_gain,
    w_query,
    w_key,
    w_value,
    q_gain,
    k_gain,
    w_out,
    post_gain,
    w_gate,
    w_up,
    w_down,
    cotangent,
):
    count = lax.axis_size(AXES)
    orders = bit_orders(count)
    ctx_order = list(range(lax.axis_size("ctx").bit_length() - 1))
    gains = jnp.concatenate([in_gain, q_gain, k_gain, post_gain])
    gain_width = -(-gains.shape[0] // 128) * 128
    gains = jnp.pad(gains, (0, gain_width - gains.shape[0]))
    gains = gather_all(gains[None, :], AXES, orders[0])
    cuts = [in_gain.shape[0], q_gain.shape[0], k_gain.shape[0], post_gain.shape[0]]
    ends = [sum(cuts[: i + 1]) for i in range(4)]
    gain_one, qgain_full, kgain_full, gain_two = [
        gains[:, end - cut : end].reshape(-1) for cut, end in zip(cuts, ends)
    ]
    query_mat = gather_all(w_query, AXES, orders[1])
    key_mat = gather_all(w_key, AXES, orders[2])
    value_mat = gather_all(w_value, AXES, orders[0])
    out_mat = gather_all(w_out, AXES, orders[0])
    gate_mat = gather_all(w_gate, AXES, orders[1])
    up_mat = gather_all(w_up, AXES, orders[2])
    down_mat = gather_all(w_down, AXES, orders[0])
    seq_count, local_len, model_width = tokens.shape
    seq_len = local_len * lax.axis_size("ctx")
    head_dim = qgain_full.shape[0]
    kv_heads = key_mat.shape[1] // head_dim
    q_heads = query_mat.shape[1] // head_dim
    group_size = q_heads // kv_heads
    kv_width = kv_heads * head_dim
    row_count = seq_count * local_len
    score_scale = head_dim ** (-0.5)
    local_pos = lax.axis_index("ctx") * local_len + jnp.arange(local_len, dtype=jnp.int32)
    key_pos = jnp.arange(seq_len, dtype=jnp.int32)
    q_segment, q_relative = doc_layout(doc_lengths, local_pos)
    k_segment = doc_layout(doc_lengths, key_pos)[0]
    gain_in = gain_one.astype(jnp.float32)
    gain_query = qgain_full.astype(jnp.float32)
    gain_key = kgain_full.astype(jnp.float32)
    gain_post = gain_two.astype(jnp.float32)
    inputs = tokens.reshape(row_count, model_width).astype(jnp.float32)
    normed, inverse_one = norm_forward(inputs, gain_in)
    normed_low = normed.astype(jnp.bfloat16)
    queries = jnp.dot(normed_low, query_mat, preferred_element_type=jnp.float32).reshape(
        seq_count, local_len, q_heads, head_dim
    )
    key_pre = jnp.dot(normed_low, key_mat, preferred_element_type=jnp.float32).reshape(
        seq_count, local_len, kv_heads, head_dim
    )
    values_low = (
        jnp.dot(normed_low, value_mat, preferred_element_type=jnp.float32)
        .astype(jnp.bfloat16)
        .reshape(seq_count, local_len, kv_width)
    )
    cosine_table, sine_table = rope_tables(q_relative, head_dim)
    cosine_table = cosine_table[:, :, None, :]
    sine_table = sine_table[:, :, None, :]
    q_normed, q_inverse = norm_forward(queries, gain_query)
    q_low = rotate(q_normed, cosine_table, sine_table).astype(jnp.bfloat16)
    k_normed, k_inverse = norm_forward(key_pre, gain_key)
    k_low = (
        rotate(k_normed, cosine_table, sine_table)
        .astype(jnp.bfloat16)
        .reshape(seq_count, local_len, kv_width)
    )
    key_all = [gather_all(k_low[i], "ctx", ctx_order) for i in range(seq_count)]
    value_all = [gather_all(values_low[i], "ctx", ctx_order) for i in range(seq_count)]

    def block_scores(q_seq, k_seq, q_seg, k_seg, k_positions):
        grouped = q_seq.reshape(local_len, kv_heads, group_size, head_dim)
        key_heads = k_seq.reshape(k_seq.shape[0], kv_heads, head_dim)
        scores = score_scale * jnp.einsum(
            "qkgd,skd->kgqs", grouped, key_heads, preferred_element_type=jnp.float32
        )
        allowed = (q_seg[:, None] == k_seg[None, :]) & (k_positions[None, :] <= local_pos[:, None])
        return (jnp.where(allowed, scores, NEGATIVE), grouped, key_heads)

    def attend(seq_item):
        q_seq, k_seq, v_seq, q_seg, k_seg = seq_item
        scores, grouped, key_heads = block_scores(q_seq, k_seq, q_seg, k_seg, key_pos)
        value_heads = v_seq.reshape(seq_len, kv_heads, head_dim)
        row_peak = jnp.max(scores, axis=-1, keepdims=True)
        exp_scores = jnp.exp(scores - row_peak)
        row_total = jnp.sum(exp_scores, axis=-1, keepdims=True)
        probs_low = (exp_scores / row_total).astype(jnp.bfloat16)
        attended = jnp.einsum(
            "kgqs,skd->qkgd", probs_low, value_heads, preferred_element_type=jnp.float32
        )
        return (
            attended.reshape(local_len, q_heads * head_dim).astype(jnp.bfloat16),
            row_peak + jnp.log(row_total),
        )

    forward = [
        attend((q_low[i], key_all[i], value_all[i], q_segment[i], k_segment[i]))
        for i in range(seq_count)
    ]
    log_totals = [item[1] for item in forward]
    attended_flat = jnp.concatenate([item[0] for item in forward], axis=0)
    resid = inputs + jnp.dot(attended_flat, out_mat, preferred_element_type=jnp.float32)
    normed_two, inverse_two = norm_forward(resid, gain_post)
    normed_two_low = normed_two.astype(jnp.bfloat16)
    gate_pre = jnp.dot(normed_two_low, gate_mat, preferred_element_type=jnp.float32)
    up_pre = jnp.dot(normed_two_low, up_mat, preferred_element_type=jnp.float32)
    gate_sigmoid = jax.nn.sigmoid(gate_pre)
    gate_silu = gate_pre * gate_sigmoid
    hidden_low = (gate_silu * up_pre).astype(jnp.bfloat16)
    mixed = (resid + jnp.dot(hidden_low, down_mat, preferred_element_type=jnp.float32)).astype(
        jnp.bfloat16
    )
    grad_low = cotangent.reshape(row_count, model_width)
    w_down_grad = lead_product(hidden_low, grad_low)
    hidden_grad = tail_product(grad_low, down_mat)
    gate_grad = (
        hidden_grad * up_pre * gate_sigmoid * (1.0 + gate_pre * (1.0 - gate_sigmoid))
    ).astype(jnp.bfloat16)
    up_grad = (hidden_grad * gate_silu).astype(jnp.bfloat16)
    w_gate_grad = lead_product(normed_two_low, gate_grad)
    w_up_grad = lead_product(normed_two_low, up_grad)
    mlp_terms = [
        grad.astype(jnp.bfloat16) for grad in (w_down_grad, w_gate_grad, w_up_grad)
    ]
    mlp_terms, gate_grad, up_grad = lax.optimization_barrier((mlp_terms, gate_grad, up_grad))
    mlp_terms = step_all(mlp_terms, orders, 0)
    normed_two_grad = tail_product(gate_grad, gate_mat) + tail_product(up_grad, up_mat)
    resid_norm_grad, post_gain_grad = norm_backward(
        resid, inverse_two, gain_two.astype(jnp.float32), normed_two_grad
    )
    resid_grad = grad_low.astype(jnp.float32) + resid_norm_grad
    resid_low = resid_grad.astype(jnp.bfloat16)
    mlp_terms, resid_low = lax.optimization_barrier((mlp_terms, resid_low))
    mlp_terms = step_all(mlp_terms, orders, 1)
    mlp_step = 2
    out_terms = [lead_product(attended_flat, resid_low).astype(jnp.bfloat16)]
    out_step = 0
    attended_grad = (
        tail_product(resid_low, out_mat)
        .astype(jnp.bfloat16)
        .reshape(seq_count, local_len, q_heads * head_dim)
    )

    def score_terms(q_seq, k_seq, v_seq, q_seg, k_seg, k_positions, log_total, grad_seq):
        scores, grouped, key_heads = block_scores(q_seq, k_seq, q_seg, k_seg, k_positions)
        value_heads = v_seq.reshape(k_seq.shape[0], kv_heads, head_dim)
        attn_probs = jnp.exp(scores - log_total)
        grad_heads = grad_seq.reshape(local_len, kv_heads, group_size, head_dim)
        prob_grad = jnp.einsum(
            "qkgd,skd->kgqs", grad_heads, value_heads, preferred_element_type=jnp.float32
        )
        return (attn_probs, prob_grad, grouped, key_heads, grad_heads)

    def attend_back(seq_item):
        q_seq, k_seq, v_seq, q_seg, k_seg, log_total, grad_seq = seq_item
        attn_probs, prob_grad, grouped, key_heads, grad_heads = score_terms(
            q_seq, k_seq, v_seq, q_seg, k_seg, key_pos, log_total, grad_seq
        )
        probs_low = attn_probs.astype(jnp.bfloat16)
        row_dot = jnp.sum(attn_probs * prob_grad, axis=-1, keepdims=True)
        score_grad = (attn_probs * (prob_grad - row_dot)).astype(jnp.bfloat16)
        query_grad = score_scale * jnp.einsum(
            "kgqs,skd->qkgd", score_grad, key_heads, preferred_element_type=jnp.float32
        )
        key_grad = score_scale * jnp.einsum(
            "kgqs,qkgd->skd", score_grad, grouped, preferred_element_type=jnp.float32
        )
        value_grad = jnp.einsum(
            "kgqs,qkgd->skd", probs_low, grad_heads, preferred_element_type=jnp.float32
        )
        return (
            query_grad.reshape(local_len, q_heads, head_dim),
            key_grad.reshape(seq_len, kv_width),
            value_grad.reshape(seq_len, kv_width),
        )

    last_step = len(orders[0]) - 1
    backward = []
    for i in range(seq_count):
        grad_seq = attended_grad[i]
        if i > 0:
            mlp_terms, out_terms, grad_seq, backward[-1] = lax.optimization_barrier(
                (mlp_terms, out_terms, grad_seq, backward[-1])
            )
            if mlp_step < last_step:
                mlp_terms = step_all(mlp_terms, orders, mlp_step)
                mlp_step += 1
            if out_step < last_step:
                out_terms = step_all(out_terms, orders[:1], out_step)
                out_step += 1
        backward.append(
            attend_back(
                (
                    q_low[i],
                    key_all[i],
                    value_all[i],
                    q_segment[i],
                    k_segment[i],
                    log_totals[i],
                    grad_seq,
                )
            )
        )
    mlp_terms, out_terms, backward[-1] = lax.optimization_barrier(
        (mlp_terms, out_terms, backward[-1])
    )
    if mlp_step < last_step:
        mlp_terms = step_all(mlp_terms, orders, mlp_step)
        mlp_step += 1
    if out_step < last_step:
        out_terms = step_all(out_terms, orders[:1], out_step)
        out_step += 1
    q_rot_grad = jnp.stack([item[0] for item in backward])
    key_part, value_part = [
        jnp.stack(
            [scatter_sum(item[j].astype(jnp.bfloat16), "ctx", ctx_order) for item in backward]
        )
        for j in (1, 2)
    ]
    q_pre_grad, q_gain_grad = norm_backward(
        queries,
        q_inverse,
        qgain_full.astype(jnp.float32),
        unrotate(q_rot_grad, cosine_table, sine_table),
    )
    k_rot_grad = key_part.reshape(seq_count, local_len, kv_heads, head_dim)
    k_pre_grad, k_gain_grad = norm_backward(
        key_pre,
        k_inverse,
        kgain_full.astype(jnp.float32),
        unrotate(k_rot_grad, cosine_table, sine_table),
    )
    queries_grad = q_pre_grad.astype(jnp.bfloat16).reshape(row_count, q_heads * head_dim)
    mlp_terms, out_terms, queries_grad = lax.optimization_barrier(
        (mlp_terms, out_terms, queries_grad)
    )
    keys_grad = k_pre_grad.astype(jnp.bfloat16).reshape(row_count, kv_width)
    values_low_grad = value_part.astype(jnp.bfloat16).reshape(row_count, kv_width)
    w_query_grad = lead_product(normed_low, queries_grad)
    w_key_grad = lead_product(normed_low, keys_grad)
    w_value_grad = lead_product(normed_low, values_low_grad)
    normed_grad = (
        tail_product(queries_grad, query_mat)
        + tail_product(keys_grad, key_mat)
        + tail_product(values_low_grad, value_mat)
    )
    input_norm_grad, in_gain_grad = norm_backward(
        inputs, inverse_one, gain_one.astype(jnp.float32), normed_grad
    )
    tokens_grad = (resid_grad + input_norm_grad).reshape(seq_count, local_len, model_width)
    gain_terms = jnp.concatenate(
        [
            part.reshape(count, -1)
            for part in (in_gain_grad, q_gain_grad, k_gain_grad, post_gain_grad)
        ],
        axis=1,
    )
    gain_terms = jnp.pad(gain_terms, ((0, 0), (0, gain_width - gain_terms.shape[1])))
    gain_sums = scatter_sum(gain_terms, AXES, orders[0])[0]
    in_gain_sum, q_gain_sum, k_gain_sum, post_gain_sum = [
        gain_sums[end - cut : end] for cut, end in zip(cuts, ends)
    ]
    return (
        mixed.reshape(seq_count, local_len, model_width),
        tokens_grad,
        in_gain_sum,
        scatter_sum(w_query_grad.astype(jnp.bfloat16), AXES, orders[1]),
        scatter_sum(w_key_grad.astype(jnp.bfloat16), AXES, orders[2]),
        scatter_sum(w_value_grad.astype(jnp.bfloat16), AXES, orders[0]),
        q_gain_sum,
        k_gain_sum,
        scatter_sum(out_terms[0], AXES, orders[0], out_step),
        post_gain_sum,
        scatter_sum(mlp_terms[1], AXES, orders[1], mlp_step),
        scatter_sum(mlp_terms[2], AXES, orders[2], mlp_step),
        scatter_sum(mlp_terms[0], AXES, orders[0], mlp_step),
    )


def solution(mesh):
    placed = (
        P("dp", "ctx", None),
        P("dp", None),
        P(("dp", "ctx")),
        P(("dp", "ctx"), None),
        P(("dp", "ctx"), None),
        P(("dp", "ctx"), None),
        P(("dp", "ctx")),
        P(("dp", "ctx")),
        P(("dp", "ctx"), None),
        P(("dp", "ctx")),
        P(("dp", "ctx"), None),
        P(("dp", "ctx"), None),
        P(("dp", "ctx"), None),
        P("dp", "ctx", None),
    )
    return jax.shard_map(
        local,
        mesh=mesh,
        in_specs=placed,
        out_specs=(
            P("dp", "ctx", None),
            P("dp", "ctx", None),
            P(("dp", "ctx")),
            P(("dp", "ctx"), None),
            P(("dp", "ctx"), None),
            P(("dp", "ctx"), None),
            P(("dp", "ctx")),
            P(("dp", "ctx")),
            P(("dp", "ctx"), None),
            P(("dp", "ctx")),
            P(("dp", "ctx"), None),
            P(("dp", "ctx"), None),
            P(("dp", "ctx"), None),
        ),
        check_vma=False,
    )
```
